32 devices in a mesh: groups: 2 (over x), wide: 16 (over z, y, core).
Axes of the slice: x: 2, y: 2, z: 4, core: 2. Of those that a mesh axis runs over, the one named last changes fastest.
Arguments:
- hidden_in: bfloat16 [512, 16384], P('groups', 'wide'), parts along dimension 0, may hold values from -100 to 100
- query_values: bfloat16 [16384, 8192], P('wide'), may hold values from -0.046875 to 0.046875
- query_scales: float32 [1024, 8192], P('wide'), may hold values from 0.5 to 2
- pair_values: bfloat16 [16384, 1024], P('wide'), may hold values from -0.046875 to 0.046875
- pair_scales: float32 [1024, 1024], P('wide'), may hold values from 0.5 to 2
- output_values: bfloat16 [8192, 16384], P('wide'), may hold values from -0.0625 to 0.0625
- output_scales: float32 [512, 16384], P('wide'), may hold values from 0.5 to 2
- tensor_scales: float32 [4], replicated, may hold values from 0.6 to 1.6
Outputs:
- attended_out: bfloat16 [512, 16384], P('groups', 'wide'), parts along dimension 0
The draws below stay inside these ranges and needn't reach their ends.
There are 2 independent parts, one for each index of `groups`. The reference program is written for one: setup_inputs(seed, part) draws one part's arguments, and reference() takes and returns one part's arrays. A program takes and returns all parts, laid end to end along the dimension named above; an argument that names none is the same for every part. Nothing has to cross between parts.
All inputs are finite; a program needn't handle non-finite values.
Results may differ from the reference program's by a relative error of at most 0.012.
The reference program's roundings to bfloat16 on the way count: a program that leaves them out, or rounds other values in their place, can miss the bound.
Values may be sent and summed in bfloat16 or wider, within the bound.
A program may use at most 192 MiB of HBM per device.

```python
import math
import jax
import jax.numpy as jnp
from jax import lax

D = 16384
HEADS = 64
KV_HEADS = 4
HEAD_DIM = 128
TOKENS = 256
QW = 8192
KVW = 1024


def draw_hidden_in(key, part):
    key = jax.random.fold_in(key, 11)
    first = jax.random.fold_in(key, 0)
    base = jnp.clip(jax.random.normal(first, (TOKENS, D), jnp.float32), -4.0, 4.0)
    return base.astype(jnp.bfloat16)


def block_scale(rng, extent, cuts, least, high):
    level, own = 1.0, jax.random.fold_in(rng, 6)
    for dim, shards_of in cuts:
        steps = jnp.exp(jax.random.uniform(jax.random.fold_in(own, dim), (shards_of,), jnp.float32, least / len(cuts), high / len(cuts)))
        level = level * jnp.repeat(steps, extent[dim] // shards_of).reshape([-1 if axis == dim else 1 for axis in range(len(extent))])
    return level


def centred(key, dims, width, most, cuts=(), kind=jnp.bfloat16):
    values = width * jax.random.normal(key, dims, jnp.float32)
    if cuts:
        values = values * block_scale(key, dims, cuts, -0.22, 0.18)
    return jnp.clip(values, -most, most).astype(kind)


def setup_inputs(seed: int = 0, part: int = 0) -> dict:
    key_of = jax.random.split(jax.random.key(seed), 9)
    part_splits = jax.random.split(jax.random.fold_in(key_of[8], part), 9)
    hidden_in = draw_hidden_in(jax.random.fold_in(jax.random.fold_in(key_of[8], part), 71), part)
    query_values = centred(key_of[1], (D, QW), D ** -0.5, 0.046875, ((0, 16),))
    query_scales = jnp.clip(jnp.exp(math.log(2.0) - 1.3862944 * jax.random.uniform(key_of[2], (D // 16, QW), jnp.float32) ** block_scale(key_of[2], (D // 16, QW), ((0, 16),), -0.2, 0.2)), 0.5, 2.0)
    pair_values = centred(key_of[3], (D, KVW), D ** -0.5, 0.046875, ((0, 16),))
    pair_scales = jnp.clip(jnp.exp(math.log(2.0) - 1.3862944 * jax.random.uniform(key_of[4], (D // 16, KVW), jnp.float32) ** block_scale(key_of[4], (D // 16, KVW), ((0, 16),), -0.2, 0.2)), 0.5, 2.0)
    output_values = centred(key_of[5], (QW, D), QW ** -0.5, 0.0625, ((0, 16),))
    output_scales = jnp.clip(jnp.exp(math.log(2.0) - 1.3862944 * jax.random.uniform(key_of[6], (QW // 16, D), jnp.float32) ** block_scale(key_of[6], (QW // 16, D), ((0, 16),), -0.2, 0.2)), 0.5, 2.0)
    tensor_scales = jnp.clip(jnp.exp(jax.random.uniform(key_of[7], (4,), jnp.float32, math.log(0.6), math.log(1.6))), 0.6, 1.6)
    return dict(hidden_in=hidden_in, query_values=query_values, query_scales=query_scales, pair_values=pair_values, pair_scales=pair_scales, output_values=output_values, output_scales=output_scales, tensor_scales=tensor_scales)


def dequantize(values, scales):
    expanded = jnp.repeat(scales, 16, axis=0)
    return (values.astype(jnp.float32) * expanded).astype(jnp.bfloat16)

def full_product(left, weight):
    return jnp.dot(left, weight, preferred_element_type=jnp.float32)

def rotary_angles(head_dim, length):
    half = head_dim // 2
    freq = jnp.exp(jnp.arange(half, dtype=jnp.float32) * (-2.0 * math.log(500000.0) / head_dim))
    position = jnp.arange(length, dtype=jnp.float32)
    return position[:, None] * freq[None, :]

def rotate_last(field):
    half = field.shape[-1] // 2
    angle = rotary_angles(field.shape[-1], field.shape[0])
    cosine = jnp.cos(angle)[:, None, :]
    sine = jnp.sin(angle)[:, None, :]
    lower = field[..., :half]
    upper = field[..., half:]
    return jnp.concatenate([lower * cosine - upper * sine, upper * cosine + lower * sine], axis=-1)

def reference(hidden_in, query_values, query_scales, pair_values, pair_scales, output_values, output_scales, tensor_scales):
    query = full_product(hidden_in, dequantize(query_values, query_scales)) * tensor_scales[0]
    pair = full_product(hidden_in, dequantize(pair_values, pair_scales))
    half_width = KVW // 2
    keys = pair[:, :half_width] * tensor_scales[1]
    values_raw = pair[:, half_width:] * tensor_scales[2]
    query = rotate_last(query.reshape(TOKENS, HEADS, HEAD_DIM)).astype(jnp.bfloat16)
    keys = rotate_last(keys.reshape(TOKENS, KV_HEADS, HEAD_DIM)).astype(jnp.bfloat16)
    values = values_raw.reshape(TOKENS, KV_HEADS, HEAD_DIM).astype(jnp.bfloat16)
    share = HEADS // KV_HEADS
    keys = jnp.repeat(keys, share, axis=1)
    values = jnp.repeat(values, share, axis=1)
    scores = jnp.einsum('qhd,khd->hqk', query.astype(jnp.float32), keys.astype(jnp.float32)) / math.sqrt(HEAD_DIM)
    causal = jnp.arange(TOKENS)[:, None] >= jnp.arange(TOKENS)[None, :]
    scores = jnp.where(causal[None], scores, -1e+30)
    top = lax.optimization_barrier(jnp.max(scores, axis=-1, keepdims=True))
    expo = jnp.exp(scores - top)
    weights = (expo / lax.optimization_barrier(jnp.sum(expo, axis=-1, keepdims=True))).astype(jnp.bfloat16)
    mixed = jnp.einsum('hqk,khd->qhd', weights.astype(jnp.float32), values.astype(jnp.float32))
    mixed = mixed.reshape(TOKENS, QW).astype(jnp.bfloat16)
    result = full_product(mixed, dequantize(output_values, output_scales)) * tensor_scales[3]
    return result.astype(jnp.bfloat16)
```

```python
import functools
import math

import jax
import jax.numpy as jnp
import numpy as np
from jax import lax
from jax.experimental import pallas as pl
from jax.experimental.pallas import tpu as pltpu
from jax.sharding import PartitionSpec as P

HEADS = 64
KV_HEADS = 4
HEAD_DIM = 128
MESH = pl.DeviceIdType.MESH
F32 = jnp.float32
BF16 = jnp.bfloat16
TILES = 3
SIBLING_SLOTS = 3


def div(a, b):
    return lax.div(a, jnp.int32(b)) if not isinstance(a, int) else a // b


def rem(a, b):
    return lax.rem(a, jnp.int32(b)) if not isinstance(a, int) else a % b


def at_least_zero(a, big):
    return div(a + big, big)


def line_order(z, length, j):
    high = div(2 * z, length)
    low = z + high * (length - 1 - 2 * z)
    far = length - 1 - 2 * low
    m = j - far
    later = at_least_zero(m, 4 * length)
    m = m * later
    odd = rem(m, 2)
    near = div(m, 2) * (1 - 2 * odd) + odd * 2 * low
    place = later * near + (1 - later) * (length - 1 - j)
    return place + high * (length - 1 - 2 * place)


def rotary_tables(length):
    half = HEAD_DIM // 2
    freq = np.exp(np.arange(half, dtype=np.float32) * np.float32(-2.0 * math.log(500000.0) / HEAD_DIM))
    angle = np.arange(length, dtype=np.float32)[:, None] * freq.astype(np.float32)[None, :]
    angle = angle.astype(np.float64)
    cosine, sine = np.cos(angle), np.sin(angle)
    return (
        np.concatenate([cosine, cosine], axis=1).astype(np.float32),
        np.concatenate([-sine, sine], axis=1).astype(np.float32),
    )


def block_kernel(
    devices, length, rows_y,
    hidden, query_values, query_scales, pair_values, pair_scales, output_values, output_scales,
    tensor_scales, cosine, sine,
    out,
    tiles, tile_scales, tile_sem, tile_scales_sem, dequantized, acc,
    pair_buf, pair_scales_buf, pair_sem, kv_part,
    out_weight, out_scales, out_sem,
    a_send, a_recv, a_ysend, a_yrecv, a_own, a_up, a_down,
    a_ss, a_sr, a_ys, a_yr, a_zs, a_ur, a_dr,
    b_send, b_recv, b_ysend, b_yrecv, b_own, b_up, b_down,
    b_ss, b_sr, b_ys, b_yr, b_zs, b_ur, b_dr,
    kv_all, kv_send_sem, kv_recv_sem, keys, values, mixed,
):
    tokens, depth = hidden.shape
    block_a = query_values.shape[1] // devices
    block_b = output_values.shape[1] // devices
    depth_b = output_values.shape[0]
    sharers = devices // KV_HEADS
    half = pair_values.shape[1] // 2
    share_rows = tokens // sharers
    fold = block_a // (2 * HEAD_DIM)
    extra = share_rows // fold
    cells = length * rows_y
    steps = 2 * cells

    me = lax.axis_index("wide")
    core = rem(me, 2)
    y = rem(div(me, 2), rows_y)
    z = div(me, 2 * rows_y)
    share = rem(me, sharers)
    sibling = me + 1 - 2 * core
    across = me + 2 * (1 - 2 * y) if rows_y == 2 else me
    stride = 2 * rows_y

    def cell_device(k, owner_core):
        zt = line_order(z, length, rem(k, length))
        yt = rem(y + 1 + div(k, length), 2) if rows_y == 2 else y
        return (zt * rows_y + yt) * 2 + owner_core

    def step_info(t):
        odd = rem(t, 2)
        first = div(steps - t, steps)
        last = div(t + 1, steps)
        for_sibling = first + odd * (1 - last)
        k = div(t - 1 + 2 * for_sibling, 2)
        return for_sibling, k, cell_device(k, core + for_sibling * (1 - 2 * core))

    def tile_copies(t):
        _, _, dest = step_info(t)
        slot = rem(t, TILES)
        columns = pl.ds(pl.multiple_of(dest * block_a, block_a), block_a)
        return (
            pltpu.make_async_copy(query_values.at[:, columns], tiles.at[slot], tile_sem.at[slot]),
            pltpu.make_async_copy(query_scales.at[:, columns], tile_scales.at[slot], tile_scales_sem.at[slot]),
        )

    pair_copies = (
        pltpu.make_async_copy(pair_values, pair_buf, pair_sem.at[0]),
        pltpu.make_async_copy(pair_scales, pair_scales_buf, pair_sem.at[1]),
    )
    part_b = output_values.shape[1] // length

    def out_copies(j):
        columns = pl.ds(pl.multiple_of(j * part_b, part_b), part_b)
        return (
            pltpu.make_async_copy(output_values.at[:, columns], out_weight.at[:, columns], out_sem.at[0, j]),
            pltpu.make_async_copy(output_scales.at[:, columns], out_scales.at[:, columns], out_sem.at[1, j]),
        )

    for copy in pair_copies:
        copy.start()
    for t in range(TILES - 1):
        for copy in tile_copies(jnp.int32(t)):
            copy.start()

    barrier = pltpu.get_barrier_semaphore()

    def greet(device):
        pl.semaphore_signal(barrier, inc=1, device_id={"wide": device}, device_id_type=MESH)

    for i in range(1, sharers):
        greet(me - share + rem(share + i, sharers))

    @pl.when(z > 0)
    def _():
        greet(me - stride)

    @pl.when(z < length - 1)
    def _():
        greet(me + stride)

    def dequantize(source, scales, target, count, column, width, wide_column):
        for r in range(count):
            rows = pl.ds(16 * r, 16)
            scaled = source[rows, pl.ds(wide_column, width)].astype(F32) * scales[pl.ds(r, 1), pl.ds(wide_column, width)]
            target[rows, pl.ds(column, width)] = scaled.astype(BF16)

    for copy in pair_copies:
        copy.wait()

    @pl.loop(0, 2 * half // 256)
    def _(i):
        column = pl.multiple_of(i * 256, 256)
        dequantize(pair_buf, pair_scales_buf, dequantized, depth // 16, 0, 256, column)
        product = jnp.dot(hidden[...], dequantized[:, :256], preferred_element_type=F32)
        part = div(i, half // 256)
        head = 2 * rem(i, half // 256)
        into = pl.ds(pl.multiple_of(part * HEAD_DIM, HEAD_DIM), HEAD_DIM)
        kv_part[head, :, into] = product[:, :HEAD_DIM]
        kv_part[head + 1, :, into] = product[:, HEAD_DIM:]

    pl.semaphore_wait(
        barrier, sharers - 1 + jnp.minimum(z, 1) + jnp.minimum(length - 1 - z, 1)
    )

    def remote(source, target, send_sem, recv_sem, device):
        return pltpu.make_async_remote_copy(
            src_ref=source, dst_ref=target, send_sem=send_sem, recv_sem=recv_sem,
            device_id={"wide": device}, device_id_type=MESH,
        )

    def reduce_scatter(multiply, rows, width, between, bufs):
        send, recv, ysend, yrecv, own, up, down, ss, sr, ys, yr, zs, ur, dr = bufs
        block = acc.at[pl.ds(0, rows), pl.ds(0, width)]

        def to_sibling(k):
            slot = rem(k, SIBLING_SLOTS)
            return remote(send.at[slot], recv.at[k], ss.at[slot], sr.at[k], sibling)

        def to_across(j):
            return remote(ysend.at[j], yrecv.at[j], ys.at[j], yr.at[j], across)

        @pl.loop(0, steps)
        def _(t):
            for_sibling, k, dest = step_info(t)
            multiply(t, dest)

            @pl.when(for_sibling == 1)
            def _():
                @pl.when(k >= SIBLING_SLOTS)
                def _():
                    to_sibling(k - SIBLING_SLOTS).wait_send()

                send[rem(k, SIBLING_SLOTS)] = block[...].astype(BF16)
                to_sibling(k).start()

            @pl.when(for_sibling == 0)
            def _():
                to_sibling(k).wait_recv()
                if rows_y == 2:
                    @pl.when(k < length)
                    def _():
                        ysend[k] = (block[...] + recv[k].astype(F32)).astype(BF16)
                        to_across(k).start()

                    @pl.when(k >= length)
                    def _():
                        own[k - length] = block[...] + recv[k].astype(F32)
                else:
                    own[k] = block[...] + recv[k].astype(F32)

        for k in range(cells - SIBLING_SLOTS, cells):
            to_sibling(k).wait_send()

        def to_up(j, zt):
            return remote(yrecv.at[j], up.at[zt], zs.at[j], ur.at[zt], me + stride)

        def to_down(j, zt):
            return remote(yrecv.at[j], down.at[zt], zs.at[j], dr.at[zt], me - stride)

        def collect(j):
            if rows_y == 2:
                to_across(j).wait_recv()
                own[j] = own[j] + yrecv[j].astype(F32)

        def from_below(j, zt):
            @pl.when(z > 0)
            def _():
                to_up(0, zt).wait_recv()
                own[j] = own[j] + up[zt].astype(F32)

        def from_above(j, zt):
            @pl.when(z < length - 1)
            def _():
                to_down(0, zt).wait_recv()
                own[j] = own[j] + down[zt].astype(F32)

        @pl.loop(0, length - 1)
        def _(j):
            between(j)
            zt = line_order(z, length, j)
            collect(j)

            @pl.when(zt > z)
            def _():
                from_below(j, zt)
                yrecv[j] = own[j].astype(BF16)
                to_up(j, zt).start()

            @pl.when(zt < z)
            def _():
                from_above(j, zt)
                yrecv[j] = own[j].astype(BF16)
                to_down(j, zt).start()

        between(length - 1)
        collect(length - 1)
        from_below(length - 1, z)
        from_above(length - 1, z)

        def settle():
            for j in range(length - 1):
                to_up(j, z).wait_send()
            if rows_y == 2:
                for j in range(length):
                    to_across(j).wait_send()

        return own.at[length - 1], settle

    def multiply_a(t, dest):
        @pl.when(t + TILES - 1 < steps)
        def _():
            for copy in tile_copies(t + TILES - 1):
                copy.start()

        for copy in tile_copies(t):
            copy.wait()
        slot = rem(t, TILES)
        dequantize(tiles.at[slot], tile_scales.at[slot], dequantized, depth // 16, 0, block_a, 0)
        acc[:tokens, :block_a] = jnp.dot(hidden[...], dequantized[:, :block_a], preferred_element_type=F32)
        head, piece = div(dest, sharers), rem(dest, sharers)
        for i in range(fold):
            first = pl.multiple_of(piece * share_rows + i * extra, extra)
            acc[tokens:tokens + extra, i * 2 * HEAD_DIM:(i + 1) * 2 * HEAD_DIM] = kv_part[head, pl.ds(first, extra), :]

        @pl.when(t == steps - TILES)
        def _():
            for j in range(length):
                for copy in out_copies(j):
                    copy.start()

    def prepare_output(j):
        for copy in out_copies(j):
            copy.wait()

        @pl.loop(0, part_b // 512)
        def _(i):
            column = pl.multiple_of(j * part_b + i * 512, 512)
            dequantize(out_weight, out_scales, out_weight, depth_b // 16, column, 512, column)

    total, settle_a = reduce_scatter(
        multiply_a, tokens + extra, block_a, prepare_output,
        (a_send, a_recv, a_ysend, a_yrecv, a_own, a_up, a_down, a_ss, a_sr, a_ys, a_yr, a_zs, a_ur, a_dr),
    )

    def to_sharer(i):
        other = rem(share + i, sharers)
        return remote(
            kv_all.at[share], kv_all.at[share], kv_send_sem.at[other], kv_recv_sem.at[share], me - share + other
        )

    def from_sharer(i):
        other = rem(share + i, sharers)
        return remote(
            kv_all.at[other], kv_all.at[other], kv_send_sem.at[other], kv_recv_sem.at[other], me - share + other
        )

    kv_all[share] = total[tokens:, :]
    for i in range(1, sharers):
        to_sharer(i).start()
    settle_a()

    def rotate(field):
        return field * cosine[...] + pltpu.roll(field, HEAD_DIM // 2, 1) * sine[...]

    local_heads = block_a // HEAD_DIM
    queries = [
        rotate(total[:tokens, h * HEAD_DIM:(h + 1) * HEAD_DIM] * tensor_scales[0]).astype(BF16)
        for h in range(local_heads)
    ]
    for i in range(1, sharers):
        from_sharer(i).wait_recv()
    for q in range(sharers):
        for i in range(fold):
            rows = slice(q * share_rows + i * extra, q * share_rows + (i + 1) * extra)
            first = i * 2 * HEAD_DIM
            keys[rows, :] = kv_all[q, :, first:first + HEAD_DIM]
            values[rows, :] = kv_all[q, :, first + HEAD_DIM:first + 2 * HEAD_DIM]
    key_rows = rotate(keys[...] * tensor_scales[1]).astype(BF16)
    value_rows = (values[...] * tensor_scales[2]).astype(BF16)
    causal = lax.broadcasted_iota(jnp.int32, (tokens, tokens), 0) >= lax.broadcasted_iota(
        jnp.int32, (tokens, tokens), 1
    )
    for h in range(local_heads):
        scores = lax.dot_general(
            queries[h], key_rows, (((1,), (1,)), ((), ())), preferred_element_type=F32
        ) / math.sqrt(HEAD_DIM)
        scores = jnp.where(causal, scores, -1e30)
        top = jnp.max(scores, axis=-1, keepdims=True)
        expo = jnp.exp(scores - top)
        weights = (expo / jnp.sum(expo, axis=-1, keepdims=True)).astype(BF16)
        mixed[:, h * HEAD_DIM:(h + 1) * HEAD_DIM] = jnp.dot(
            weights, value_rows, preferred_element_type=F32
        ).astype(BF16)
    for i in range(1, sharers):
        to_sharer(i).wait_send()

    def multiply_b(t, dest):
        columns = pl.ds(pl.multiple_of(dest * block_b, block_b), block_b)
        acc[:tokens, :block_b] = jnp.dot(mixed[...], out_weight[:, columns], preferred_element_type=F32)

    summed, settle_b = reduce_scatter(
        multiply_b, tokens, block_b, lambda j: None,
        (b_send, b_recv, b_ysend, b_yrecv, b_own, b_up, b_down, b_ss, b_sr, b_ys, b_yr, b_zs, b_ur, b_dr),
    )
    out[...] = (summed[...] * tensor_scales[3]).astype(BF16)
    settle_b()


def on_device(
    hidden_in, query_values, query_scales, pair_values, pair_scales, output_values, output_scales, tensor_scales
):
    devices = lax.axis_size("wide")
    rows_y = 2 if devices == 16 else 1
    length = devices // (2 * rows_y)
    cells = length * rows_y
    tokens, depth = hidden_in.shape
    block_a = query_values.shape[1] // devices
    block_b = output_values.shape[1] // devices
    sharers = devices // KV_HEADS
    extra = tokens // sharers // (block_a // (2 * HEAD_DIM))
    cosine, sine = rotary_tables(tokens)
    dma = pltpu.SemaphoreType.DMA

    def buffers(rows, width):
        slots_y = length if rows_y == 2 else 1
        return [
            pltpu.VMEM((SIBLING_SLOTS, rows, width), BF16),
            pltpu.VMEM((cells, rows, width), BF16),
            pltpu.VMEM((slots_y, rows, width) if rows_y == 2 else (1, 16, 128), BF16),
            pltpu.VMEM((length, rows, width), BF16),
            pltpu.VMEM((length, rows, width), F32),
            pltpu.VMEM((length, rows, width), BF16),
            pltpu.VMEM((length, rows, width), BF16),
            dma((SIBLING_SLOTS,)), dma((cells,)), dma((length,)), dma((length,)),
            dma((length,)), dma((length,)), dma((length,)),
        ]

    anywhere = pl.BlockSpec(memory_space=pl.ANY)
    vmem = pl.BlockSpec(memory_space=pltpu.VMEM)
    features = query_values.shape[1] + pair_values.shape[1]
    return pl.pallas_call(
        functools.partial(block_kernel, devices, length, rows_y),
        out_shape=jax.ShapeDtypeStruct((tokens, block_b), BF16),
        in_specs=[vmem] + [anywhere] * 6 + [pl.BlockSpec(memory_space=pltpu.SMEM), vmem, vmem],
        out_specs=vmem,
        scratch_shapes=[
            pltpu.VMEM((TILES, depth, block_a), BF16),
            pltpu.VMEM((TILES, depth // 16, block_a), F32),
            dma((TILES,)), dma((TILES,)),
            pltpu.VMEM((depth, max(block_a, 256)), BF16),
            pltpu.VMEM((tokens + extra, max(block_a, block_b)), F32),
            pltpu.VMEM(pair_values.shape, BF16),
            pltpu.VMEM(pair_scales.shape, F32),
            dma((2,)),
            pltpu.VMEM((KV_HEADS, tokens, 2 * HEAD_DIM), F32),
            pltpu.VMEM(output_values.shape, BF16),
            pltpu.VMEM(output_scales.shape, F32),
            dma((2, length)),
        ]
        + buffers(tokens + extra, block_a)
        + buffers(tokens, block_b)
        + [
            pltpu.VMEM((sharers, extra, block_a), F32),
            dma((sharers,)), dma((sharers,)),
            pltpu.VMEM((tokens, HEAD_DIM), F32),
            pltpu.VMEM((tokens, HEAD_DIM), F32),
            pltpu.VMEM((tokens, block_a), BF16),
        ],
        compiler_params=pltpu.CompilerParams(
            collective_id=0, has_side_effects=True, vmem_limit_bytes=63 * 1024 * 1024
        ),
        cost_estimate=pl.CostEstimate(
            flops=2 * tokens * (depth * features + output_values.size),
            bytes_accessed=2 * (query_values.size + pair_values.size + output_values.size),
            transcendentals=tokens * tokens * (block_a // HEAD_DIM),
        ),
    )(
        hidden_in, query_values, query_scales, pair_values, pair_scales, output_values, output_scales,
        tensor_scales, jnp.asarray(cosine), jnp.asarray(sine),
    )


def solution(mesh):
    in_specs = (P("groups", "wide"),) + (P("wide", None),) * 6 + (P(),)
    return jax.shard_map(
        on_device, mesh=mesh, in_specs=in_specs, out_specs=P("groups", "wide"), check_vma=False
    )
```

```python
import functools
import math

import jax
import jax.numpy as jnp
import numpy as np
from jax import lax
from jax.experimental import pallas as pl
from jax.experimental.pallas import tpu as pltpu
from jax.sharding import PartitionSpec as P

HEADS = 64
KV_HEADS = 4
HEAD_DIM = 128
MESH = pl.DeviceIdType.MESH
F32 = jnp.float32
BF16 = jnp.bfloat16
TILES = 3
SIBLING_SLOTS = 3


def div(a, b):
    return lax.div(a, jnp.int32(b)) if not isinstance(a, int) else a // b


def rem(a, b):
    return lax.rem(a, jnp.int32(b)) if not isinstance(a, int) else a % b


def at_least_zero(a, big):
    return div(a + big, big)


def line_order(z, length, j):
    high = div(2 * z, length)
    low = z + high * (length - 1 - 2 * z)
    far = length - 1 - 2 * low
    m = j - far
    later = at_least_zero(m, 4 * length)
    m = m * later
    odd = rem(m, 2)
    near = div(m, 2) * (1 - 2 * odd) + odd * 2 * low
    place = later * near + (1 - later) * (length - 1 - j)
    return place + high * (length - 1 - 2 * place)


def rotary_tables(length):
    half = HEAD_DIM // 2
    freq = np.exp(np.arange(half, dtype=np.float32) * np.float32(-2.0 * math.log(500000.0) / HEAD_DIM))
    angle = np.arange(length, dtype=np.float32)[:, None] * freq.astype(np.float32)[None, :]
    angle = angle.astype(np.float64)
    cosine, sine = np.cos(angle), np.sin(angle)
    return (
        np.concatenate([cosine, cosine], axis=1).astype(np.float32),
        np.concatenate([-sine, sine], axis=1).astype(np.float32),
    )


def block_kernel(
    devices, length, rows_y,
    hidden, query_values, query_scales, pair_values, pair_scales, output_values, output_scales,
    tensor_scales, cosine, sine,
    out,
    tiles, tile_scales, tile_sem, tile_scales_sem, dequantized, acc,
    pair_buf, pair_scales_buf, pair_sem, kv_part,
    out_weight, out_scales, out_sem,
    a_send, a_recv, a_ysend, a_yrecv, a_own, a_zrecv,
    a_ss, a_sr, a_ys, a_yr, a_zs, a_zr,
    b_send, b_recv, b_ysend, b_yrecv, b_own, b_zrecv,
    b_ss, b_sr, b_ys, b_yr, b_zs, b_zr,
    kv_all, kv_send_sem, kv_recv_sem, keys, values, mixed,
):
    tokens, depth = hidden.shape
    block_a = query_values.shape[1] // devices
    block_b = output_values.shape[1] // devices
    depth_b = output_values.shape[0]
    sharers = devices // KV_HEADS
    half = pair_values.shape[1] // 2
    share_rows = tokens // sharers
    fold = block_a // (2 * HEAD_DIM)
    extra = share_rows // fold
    cells = length * rows_y
    steps = 2 * cells

    me = lax.axis_index("wide")
    core = rem(me, 2)
    y = rem(div(me, 2), rows_y)
    z = div(me, 2 * rows_y)
    share = rem(me, sharers)
    sibling = me + 1 - 2 * core
    across = me + 2 * (1 - 2 * y) if rows_y == 2 else me
    stride = 2 * rows_y

    def cell_device(k, owner_core):
        zt = line_order(z, length, rem(k, length))
        yt = rem(y + 1 + div(k, length), 2) if rows_y == 2 else y
        return (zt * rows_y + yt) * 2 + owner_core

    def step_info(t):
        odd = rem(t, 2)
        first = div(steps - t, steps)
        last = div(t + 1, steps)
        for_sibling = first + odd * (1 - last)
        k = div(t - 1 + 2 * for_sibling, 2)
        return for_sibling, k, cell_device(k, core + for_sibling * (1 - 2 * core))

    def tile_copies(t):
        _, _, dest = step_info(t)
        slot = rem(t, TILES)
        columns = pl.ds(pl.multiple_of(dest * block_a, block_a), block_a)
        return (
            pltpu.make_async_copy(query_values.at[:, columns], tiles.at[slot], tile_sem.at[slot]),
            pltpu.make_async_copy(query_scales.at[:, columns], tile_scales.at[slot], tile_scales_sem.at[slot]),
        )

    pair_copies = (
        pltpu.make_async_copy(pair_values, pair_buf, pair_sem.at[0]),
        pltpu.make_async_copy(pair_scales, pair_scales_buf, pair_sem.at[1]),
    )
    part_b = output_values.shape[1] // length

    def out_copies(j):
        columns = pl.ds(pl.multiple_of(j * part_b, part_b), part_b)
        return (
            pltpu.make_async_copy(output_values.at[:, columns], out_weight.at[:, columns], out_sem.at[0, j]),
            pltpu.make_async_copy(output_scales.at[:, columns], out_scales.at[:, columns], out_sem.at[1, j]),
        )

    for copy in pair_copies:
        copy.start()
    for t in range(TILES - 1):
        for copy in tile_copies(jnp.int32(t)):
            copy.start()

    barrier = pltpu.get_barrier_semaphore()

    def greet(device):
        pl.semaphore_signal(barrier, inc=1, device_id={"wide": device}, device_id_type=MESH)

    for i in range(1, sharers):
        greet(me - share + rem(share + i, sharers))

    for i in range(1, length):
        greet(me + (rem(z + i, length) - z) * stride)

    def dequantize(source, scales, target, count, column, width, wide_column):
        for r in range(count):
            rows = pl.ds(16 * r, 16)
            scaled = source[rows, pl.ds(wide_column, width)].astype(F32) * scales[pl.ds(r, 1), pl.ds(wide_column, width)]
            target[rows, pl.ds(column, width)] = scaled.astype(BF16)

    for copy in pair_copies:
        copy.wait()

    @pl.loop(0, 2 * half // 256)
    def _(i):
        column = pl.multiple_of(i * 256, 256)
        dequantize(pair_buf, pair_scales_buf, dequantized, depth // 16, 0, 256, column)
        product = jnp.dot(hidden[...], dequantized[:, :256], preferred_element_type=F32)
        part = div(i, half // 256)
        head = 2 * rem(i, half // 256)
        into = pl.ds(pl.multiple_of(part * HEAD_DIM, HEAD_DIM), HEAD_DIM)
        kv_part[head, :, into] = product[:, :HEAD_DIM]
        kv_part[head + 1, :, into] = product[:, HEAD_DIM:]

    pl.semaphore_wait(barrier, sharers + length - 2)

    def remote(source, target, send_sem, recv_sem, device):
        return pltpu.make_async_remote_copy(
            src_ref=source, dst_ref=target, send_sem=send_sem, recv_sem=recv_sem,
            device_id={"wide": device}, device_id_type=MESH,
        )

    def reduce_scatter(multiply, below, width, between, bufs):
        send, recv, ysend, yrecv, own, zrecv, ss, sr, ys, yr, zs, zr = bufs
        rows = tokens + below
        block = acc.at[pl.ds(0, rows), pl.ds(0, width)]

        def pack(target, value):
            high = value.astype(BF16)
            target[:rows, :] = high
            if below:
                target[rows:, :] = (value[tokens:] - high[tokens:].astype(F32)).astype(BF16)

        def unpack(source):
            top = source[:tokens, :].astype(F32)
            if not below:
                return top
            low = source[tokens:rows, :].astype(F32) + source[rows:, :].astype(F32)
            return jnp.concatenate([top, low], axis=0)

        def to_sibling(k):
            slot = rem(k, SIBLING_SLOTS)
            return remote(send.at[slot], recv.at[k], ss.at[slot], sr.at[k], sibling)

        def to_across(j):
            return remote(ysend.at[j], yrecv.at[j], ys.at[j], yr.at[j], across)

        @pl.loop(0, steps)
        def _(t):
            for_sibling, k, dest = step_info(t)
            multiply(t, dest)

            @pl.when(for_sibling == 1)
            def _():
                @pl.when(k >= SIBLING_SLOTS)
                def _():
                    to_sibling(k - SIBLING_SLOTS).wait_send()

                send[rem(k, SIBLING_SLOTS)] = block[...].astype(send.dtype)
                to_sibling(k).start()

            @pl.when(for_sibling == 0)
            def _():
                to_sibling(k).wait_recv()
                if rows_y == 2:
                    @pl.when(k < length)
                    def _():
                        pack(ysend.at[k], block[...] + recv[k].astype(F32))
                        to_across(k).start()

                    @pl.when(k >= length)
                    def _():
                        own[k - length] = block[...] + recv[k].astype(F32)
                else:
                    own[k] = block[...] + recv[k].astype(F32)

        for k in range(cells - SIBLING_SLOTS, cells):
            to_sibling(k).wait_send()

        def to_line(j, zt):
            return remote(yrecv.at[j], zrecv.at[z], zs.at[j], zr.at[z], me + (zt - z) * stride)

        def from_line(zf):
            return remote(yrecv.at[0], zrecv.at[zf], zs.at[0], zr.at[zf], me + (zf - z) * stride)

        def collected(j):
            if rows_y == 2:
                to_across(j).wait_recv()
                return own[j] + unpack(yrecv.at[j])
            return own[j]

        @pl.loop(0, length - 1)
        def _(j):
            between(j)
            pack(yrecv.at[j], collected(j))
            to_line(j, line_order(z, length, j)).start()

        between(length - 1)
        own[length - 1] = collected(length - 1)
        for i in range(1, length):
            zf = rem(z + i, length)
            from_line(zf).wait_recv()
            own[length - 1] = own[length - 1] + unpack(zrecv.at[zf])

        def settle():
            for j in range(length - 1):
                to_line(j, line_order(z, length, jnp.int32(j))).wait_send()
            if rows_y == 2:
                for j in range(length):
                    to_across(j).wait_send()

        return own.at[length - 1], settle

    def multiply_a(t, dest):
        @pl.when(t + TILES - 1 < steps)
        def _():
            for copy in tile_copies(t + TILES - 1):
                copy.start()

        for copy in tile_copies(t):
            copy.wait()
        slot = rem(t, TILES)
        dequantize(tiles.at[slot], tile_scales.at[slot], dequantized, depth // 16, 0, block_a, 0)
        acc[:tokens, :block_a] = jnp.dot(hidden[...], dequantized[:, :block_a], preferred_element_type=F32)
        head, piece = div(dest, sharers), rem(dest, sharers)
        for i in range(fold):
            first = pl.multiple_of(piece * share_rows + i * extra, extra)
            acc[tokens:tokens + extra, i * 2 * HEAD_DIM:(i + 1) * 2 * HEAD_DIM] = kv_part[head, pl.ds(first, extra), :]

        @pl.when(t == steps - TILES)
        def _():
            for j in range(length):
                for copy in out_copies(j):
                    copy.start()

    def prepare_output(j):
        for copy in out_copies(j):
            copy.wait()

        @pl.loop(0, part_b // 512)
        def _(i):
            column = pl.multiple_of(j * part_b + i * 512, 512)
            dequantize(out_weight, out_scales, out_weight, depth_b // 16, column, 512, column)

    total, settle_a = reduce_scatter(
        multiply_a, extra, block_a, prepare_output,
        (a_send, a_recv, a_ysend, a_yrecv, a_own, a_zrecv, a_ss, a_sr, a_ys, a_yr, a_zs, a_zr),
    )

    def to_sharer(i):
        other = rem(share + i, sharers)
        return remote(
            kv_all.at[share], kv_all.at[share], kv_send_sem.at[other], kv_recv_sem.at[share], me - share + other
        )

    def from_sharer(i):
        other = rem(share + i, sharers)
        return remote(
            kv_all.at[other], kv_all.at[other], kv_send_sem.at[other], kv_recv_sem.at[other], me - share + other
        )

    kv_all[share] = total[tokens:, :]
    for i in range(1, sharers):
        to_sharer(i).start()
    settle_a()

    def rotate(field):
        return field * cosine[...] + pltpu.roll(field, HEAD_DIM // 2, 1) * sine[...]

    local_heads = block_a // HEAD_DIM
    queries = [
        rotate(total[:tokens, h * HEAD_DIM:(h + 1) * HEAD_DIM] * tensor_scales[0]).astype(BF16)
        for h in range(local_heads)
    ]
    for i in range(1, sharers):
        from_sharer(i).wait_recv()
    for q in range(sharers):
        for i in range(fold):
            rows = slice(q * share_rows + i * extra, q * share_rows + (i + 1) * extra)
            first = i * 2 * HEAD_DIM
            keys[rows, :] = kv_all[q, :, first:first + HEAD_DIM]
            values[rows, :] = kv_all[q, :, first + HEAD_DIM:first + 2 * HEAD_DIM]
    key_rows = rotate(keys[...] * tensor_scales[1]).astype(BF16)
    value_rows = (values[...] * tensor_scales[2]).astype(BF16)
    causal = lax.broadcasted_iota(jnp.int32, (tokens, tokens), 0) >= lax.broadcasted_iota(
        jnp.int32, (tokens, tokens), 1
    )
    for h in range(local_heads):
        scores = lax.dot_general(
            queries[h], key_rows, (((1,), (1,)), ((), ())), preferred_element_type=F32
        ) / math.sqrt(HEAD_DIM)
        scores = jnp.where(causal, scores, -1e30)
        top = jnp.max(scores, axis=-1, keepdims=True)
        expo = jnp.exp(scores - top)
        weights = (expo / jnp.sum(expo, axis=-1, keepdims=True)).astype(BF16)
        mixed[:, h * HEAD_DIM:(h + 1) * HEAD_DIM] = jnp.dot(
            weights, value_rows, preferred_element_type=F32
        ).astype(BF16)
    for i in range(1, sharers):
        to_sharer(i).wait_send()

    def multiply_b(t, dest):
        columns = pl.ds(pl.multiple_of(dest * block_b, block_b), block_b)
        acc[:tokens, :block_b] = jnp.dot(mixed[...], out_weight[:, columns], preferred_element_type=F32)

    summed, settle_b = reduce_scatter(
        multiply_b, 0, block_b, lambda j: None,
        (b_send, b_recv, b_ysend, b_yrecv, b_own, b_zrecv, b_ss, b_sr, b_ys, b_yr, b_zs, b_zr),
    )
    out[...] = (summed[...] * tensor_scales[3]).astype(BF16)
    settle_b()


def on_device(
    hidden_in, query_values, query_scales, pair_values, pair_scales, output_values, output_scales, tensor_scales
):
    devices = lax.axis_size("wide")
    rows_y = 2 if devices == 16 else 1
    length = devices // (2 * rows_y)
    cells = length * rows_y
    tokens, depth = hidden_in.shape
    block_a = query_values.shape[1] // devices
    block_b = output_values.shape[1] // devices
    sharers = devices // KV_HEADS
    extra = tokens // sharers // (block_a // (2 * HEAD_DIM))
    cosine, sine = rotary_tables(tokens)
    dma = pltpu.SemaphoreType.DMA

    def buffers(below, width, sibling_type):
        rows, wire = tokens + below, tokens + 2 * below
        return [
            pltpu.VMEM((SIBLING_SLOTS, rows, width), sibling_type),
            pltpu.VMEM((cells, rows, width), sibling_type),
            pltpu.VMEM((length, wire, width) if rows_y == 2 else (1, 16, 128), BF16),
            pltpu.VMEM((length, wire, width), BF16),
            pltpu.VMEM((length, rows, width), F32),
            pltpu.VMEM((length, wire, width), BF16),
            dma((SIBLING_SLOTS,)), dma((cells,)), dma((length,)), dma((length,)),
            dma((length,)), dma((length,)),
        ]

    anywhere = pl.BlockSpec(memory_space=pl.ANY)
    vmem = pl.BlockSpec(memory_space=pltpu.VMEM)
    features = query_values.shape[1] + pair_values.shape[1]
    return pl.pallas_call(
        functools.partial(block_kernel, devices, length, rows_y),
        out_shape=jax.ShapeDtypeStruct((tokens, block_b), BF16),
        in_specs=[vmem] + [anywhere] * 6 + [pl.BlockSpec(memory_space=pltpu.SMEM), vmem, vmem],
        out_specs=vmem,
        scratch_shapes=[
            pltpu.VMEM((TILES, depth, block_a), BF16),
            pltpu.VMEM((TILES, depth // 16, block_a), F32),
            dma((TILES,)), dma((TILES,)),
            pltpu.VMEM((depth, max(block_a, 256)), BF16),
            pltpu.VMEM((tokens + extra, max(block_a, block_b)), F32),
            pltpu.VMEM(pair_values.shape, BF16),
            pltpu.VMEM(pair_scales.shape, F32),
            dma((2,)),
            pltpu.VMEM((KV_HEADS, tokens, 2 * HEAD_DIM), F32),
            pltpu.VMEM(output_values.shape, BF16),
            pltpu.VMEM(output_scales.shape, F32),
            dma((2, length)),
        ]
        + buffers(extra, block_a, F32)
        + buffers(0, block_b, BF16)
        + [
            pltpu.VMEM((sharers, extra, block_a), F32),
            dma((sharers,)), dma((sharers,)),
            pltpu.VMEM((tokens, HEAD_DIM), F32),
            pltpu.VMEM((tokens, HEAD_DIM), F32),
            pltpu.VMEM((tokens, block_a), BF16),
        ],
        compiler_params=pltpu.CompilerParams(
            collective_id=0, has_side_effects=True, vmem_limit_bytes=63 * 1024 * 1024
        ),
        cost_estimate=pl.CostEstimate(
            flops=2 * tokens * (depth * features + output_values.size),
            bytes_accessed=2 * (query_values.size + pair_values.size + output_values.size),
            transcendentals=tokens * tokens * (block_a // HEAD_DIM),
        ),
    )(
        hidden_in, query_values, query_scales, pair_values, pair_scales, output_values, output_scales,
        tensor_scales, jnp.asarray(cosine), jnp.asarray(sine),
    )


def solution(mesh):
    in_specs = (P("groups", "wide"),) + (P("wide", None),) * 6 + (P(),)
    return jax.shard_map(
        on_device, mesh=mesh, in_specs=in_specs, out_specs=P("groups", "wide"), check_vma=False
    )
```

```python
import functools
import math

import jax
import jax.numpy as jnp
import numpy as np
from jax import lax
from jax.experimental import pallas as pl
from jax.experimental.pallas import tpu as pltpu
from jax.sharding import PartitionSpec as P

HEADS = 64
KV_HEADS = 4
HEAD_DIM = 128
MESH = pl.DeviceIdType.MESH
F32 = jnp.float32
BF16 = jnp.bfloat16
TILES = 3
SIBLING_SLOTS = 3


def div(a, b):
    return lax.div(a, jnp.int32(b)) if not isinstance(a, int) else a // b


def rem(a, b):
    return lax.rem(a, jnp.int32(b)) if not isinstance(a, int) else a % b


def at_least_zero(a, big):
    return div(a + big, big)


def line_order(z, length, j):
    high = div(2 * z, length)
    low = z + high * (length - 1 - 2 * z)
    far = length - 1 - 2 * low
    m = j - far
    later = at_least_zero(m, 4 * length)
    m = m * later
    odd = rem(m, 2)
    near = div(m, 2) * (1 - 2 * odd) + odd * 2 * low
    place = later * near + (1 - later) * (length - 1 - j)
    return place + high * (length - 1 - 2 * place)


def rotary_tables(length):
    half = HEAD_DIM // 2
    freq = np.exp(np.arange(half, dtype=np.float32) * np.float32(-2.0 * math.log(500000.0) / HEAD_DIM))
    angle = np.arange(length, dtype=np.float32)[:, None] * freq.astype(np.float32)[None, :]
    angle = angle.astype(np.float64)
    cosine, sine = np.cos(angle), np.sin(angle)
    return (
        np.concatenate([cosine, cosine], axis=1).astype(np.float32),
        np.concatenate([-sine, sine], axis=1).astype(np.float32),
    )


def block_kernel(
    devices, length, rows_y,
    hidden, query_values, query_scales, pair_values, pair_scales, output_values, output_scales,
    tensor_scales, cosine, sine,
    out,
    tiles, tile_scales, tile_sem, tile_scales_sem, dequantized, acc,
    pair_buf, pair_scales_buf, pair_sem, kv_part,
    out_weight, out_scales, out_sem,
    a_send, a_recv, a_ysend, a_yrecv, a_own, a_zrecv,
    a_ss, a_sr, a_ys, a_yr, a_zs, a_zr,
    b_send, b_recv, b_ysend, b_yrecv, b_own, b_zrecv,
    b_ss, b_sr, b_ys, b_yr, b_zs, b_zr,
    kv_all, kv_send_sem, kv_recv_sem, keys, values, mixed,
):
    tokens, depth = hidden.shape
    block_a = query_values.shape[1] // devices
    block_b = output_values.shape[1] // devices
    depth_b = output_values.shape[0]
    sharers = devices // KV_HEADS
    half = pair_values.shape[1] // 2
    share_rows = tokens // sharers
    fold = block_a // (2 * HEAD_DIM)
    extra = share_rows // fold
    cells = length * rows_y
    steps = 2 * cells

    me = lax.axis_index("wide")
    core = rem(me, 2)
    y = rem(div(me, 2), rows_y)
    z = div(me, 2 * rows_y)
    share = rem(me, sharers)
    sibling = me + 1 - 2 * core
    across = me + 2 * (1 - 2 * y) if rows_y == 2 else me
    stride = 2 * rows_y

    def cell_device(k, owner_core):
        zt = line_order(z, length, rem(k, length))
        yt = rem(y + 1 + div(k, length), 2) if rows_y == 2 else y
        return (zt * rows_y + yt) * 2 + owner_core

    def step_info(t):
        odd = rem(t, 2)
        first = div(steps - t, steps)
        last = div(t + 1, steps)
        for_sibling = first + odd * (1 - last)
        k = div(t - 1 + 2 * for_sibling, 2)
        return for_sibling, k, cell_device(k, core + for_sibling * (1 - 2 * core))

    def tile_copies(t):
        _, _, dest = step_info(t)
        slot = rem(t, TILES)
        columns = pl.ds(pl.multiple_of(dest * block_a, block_a), block_a)
        return (
            pltpu.make_async_copy(query_values.at[:, columns], tiles.at[slot], tile_sem.at[slot]),
            pltpu.make_async_copy(query_scales.at[:, columns], tile_scales.at[slot], tile_scales_sem.at[slot]),
        )

    pair_copies = (
        pltpu.make_async_copy(pair_values, pair_buf, pair_sem.at[0]),
        pltpu.make_async_copy(pair_scales, pair_scales_buf, pair_sem.at[1]),
    )
    part_b = output_values.shape[1] // length

    def out_copies(j):
        columns = pl.ds(pl.multiple_of(j * part_b, part_b), part_b)
        return (
            pltpu.make_async_copy(output_values.at[:, columns], out_weight.at[:, columns], out_sem.at[0, j]),
            pltpu.make_async_copy(output_scales.at[:, columns], out_scales.at[:, columns], out_sem.at[1, j]),
        )

    for copy in pair_copies:
        copy.start()
    for t in range(TILES - 1):
        for copy in tile_copies(jnp.int32(t)):
            copy.start()

    barrier = pltpu.get_barrier_semaphore()

    def greet(device):
        pl.semaphore_signal(barrier, inc=1, device_id={"wide": device}, device_id_type=MESH)

    for i in range(1, sharers):
        greet(me - share + rem(share + i, sharers))

    for i in range(1, length):
        greet(me + (rem(z + i, length) - z) * stride)

    def dequantize(source, scales, target, count, column, width, wide_column):
        for r in range(count):
            rows = pl.ds(16 * r, 16)
            scaled = source[rows, pl.ds(wide_column, width)].astype(F32) * scales[pl.ds(r, 1), pl.ds(wide_column, width)]
            target[rows, pl.ds(column, width)] = scaled.astype(BF16)

    for copy in pair_copies:
        copy.wait()

    @pl.loop(0, 2 * half // 256)
    def _(i):
        column = pl.multiple_of(i * 256, 256)
        dequantize(pair_buf, pair_scales_buf, dequantized, depth // 16, 0, 256, column)
        product = jnp.dot(hidden[...], dequantized[:, :256], preferred_element_type=F32)
        part = div(i, half // 256)
        head = 2 * rem(i, half // 256)
        into = pl.ds(pl.multiple_of(part * HEAD_DIM, HEAD_DIM), HEAD_DIM)
        kv_part[head, :, into] = product[:, :HEAD_DIM]
        kv_part[head + 1, :, into] = product[:, HEAD_DIM:]

    pl.semaphore_wait(barrier, sharers + length - 2)

    def remote(source, target, send_sem, recv_sem, device):
        return pltpu.make_async_remote_copy(
            src_ref=source, dst_ref=target, send_sem=send_sem, recv_sem=recv_sem,
            device_id={"wide": device}, device_id_type=MESH,
        )

    def reduce_scatter(multiply, below, width, between, bufs):
        send, recv, ysend, yrecv, own, zrecv, ss, sr, ys, yr, zs, zr = bufs
        rows = tokens + below
        block = acc.at[pl.ds(0, rows), pl.ds(0, width)]

        def pack(target, value):
            high = value.astype(BF16)
            target[:rows, :] = high
            if below:
                target[rows:, :] = (value[tokens:] - high[tokens:].astype(F32)).astype(BF16)

        def unpack(source):
            top = source[:tokens, :].astype(F32)
            if not below:
                return top
            low = source[tokens:rows, :].astype(F32) + source[rows:, :].astype(F32)
            return jnp.concatenate([top, low], axis=0)

        def to_sibling(k):
            slot = rem(k, SIBLING_SLOTS)
            return remote(send.at[slot], recv.at[k], ss.at[slot], sr.at[k], sibling)

        def to_across(j):
            return remote(ysend.at[j], yrecv.at[j], ys.at[j], yr.at[j], across)

        @pl.loop(0, steps)
        def _(t):
            for_sibling, k, dest = step_info(t)
            multiply(t, dest)

            @pl.when(for_sibling == 1)
            def _():
                @pl.when(k >= SIBLING_SLOTS)
                def _():
                    to_sibling(k - SIBLING_SLOTS).wait_send()

                send[rem(k, SIBLING_SLOTS)] = block[...].astype(send.dtype)
                to_sibling(k).start()

            @pl.when(for_sibling == 0)
            def _():
                to_sibling(k).wait_recv()
                if rows_y == 2:
                    @pl.when(k < length)
                    def _():
                        pack(ysend.at[k], block[...] + recv[k].astype(F32))
                        to_across(k).start()

                    @pl.when(k >= length)
                    def _():
                        own[k - length] = block[...] + recv[k].astype(F32)
                else:
                    own[k] = block[...] + recv[k].astype(F32)

        for k in range(cells - SIBLING_SLOTS, cells):
            to_sibling(k).wait_send()

        def to_up(j, zt):
            return remote(yrecv.at[j], zrecv.at[zt], zs.at[j], zr.at[zt], me + stride)

        def to_down(j, zt):
            slot = zt + (1 - jnp.minimum(z - 1 - zt, 1)) * (length - zt)
            return remote(yrecv.at[j], zrecv.at[slot], zs.at[j], zr.at[slot], me - stride)

        def add_arrived(j, slot, device):
            remote(yrecv.at[0], zrecv.at[slot], zs.at[0], zr.at[slot], device).wait_recv()
            own[j] = own[j] + unpack(zrecv.at[slot])

        def from_below(j, zt):
            @pl.when(z > 0)
            def _():
                add_arrived(j, zt, me - stride)

        def from_above(j, slot):
            @pl.when(z < length - 1)
            def _():
                add_arrived(j, slot, me + stride)

        def collected(j):
            if rows_y == 2:
                to_across(j).wait_recv()
                return own[j] + unpack(yrecv.at[j])
            return own[j]

        @pl.loop(0, length - 1)
        def _(j):
            between(j)
            zt = line_order(z, length, j)
            own[j] = collected(j)

            @pl.when(zt > z)
            def _():
                from_below(j, zt)
                pack(yrecv.at[j], own[j])
                to_up(j, zt).start()

            @pl.when(zt < z)
            def _():
                from_above(j, zt)
                pack(yrecv.at[j], own[j])
                to_down(j, zt).start()

        between(length - 1)
        own[length - 1] = collected(length - 1)
        from_below(length - 1, z)
        from_above(length - 1, length)

        def settle():
            for j in range(length - 1):
                to_up(j, z).wait_send()
            if rows_y == 2:
                for j in range(length):
                    to_across(j).wait_send()

        return own.at[length - 1], settle

    def multiply_a(t, dest):
        @pl.when(t + TILES - 1 < steps)
        def _():
            for copy in tile_copies(t + TILES - 1):
                copy.start()

        for copy in tile_copies(t):
            copy.wait()
        slot = rem(t, TILES)
        dequantize(tiles.at[slot], tile_scales.at[slot], dequantized, depth // 16, 0, block_a, 0)
        acc[:tokens, :block_a] = jnp.dot(hidden[...], dequantized[:, :block_a], preferred_element_type=F32)
        head, piece = div(dest, sharers), rem(dest, sharers)
        for i in range(fold):
            first = pl.multiple_of(piece * share_rows + i * extra, extra)
            acc[tokens:tokens + extra, i * 2 * HEAD_DIM:(i + 1) * 2 * HEAD_DIM] = kv_part[head, pl.ds(first, extra), :]

        @pl.when(t == steps - TILES)
        def _():
            for j in range(length):
                for copy in out_copies(j):
                    copy.start()

    def prepare_output(j):
        for copy in out_copies(j):
            copy.wait()

        @pl.loop(0, part_b // 512)
        def _(i):
            column = pl.multiple_of(j * part_b + i * 512, 512)
            dequantize(out_weight, out_scales, out_weight, depth_b // 16, column, 512, column)

    total, settle_a = reduce_scatter(
        multiply_a, extra, block_a, prepare_output,
        (a_send, a_recv, a_ysend, a_yrecv, a_own, a_zrecv, a_ss, a_sr, a_ys, a_yr, a_zs, a_zr),
    )

    def to_sharer(i):
        other = rem(share + i, sharers)
        return remote(
            kv_all.at[share], kv_all.at[share], kv_send_sem.at[other], kv_recv_sem.at[share], me - share + other
        )

    def from_sharer(i):
        other = rem(share + i, sharers)
        return remote(
            kv_all.at[other], kv_all.at[other], kv_send_sem.at[other], kv_recv_sem.at[other], me - share + other
        )

    kv_all[share] = total[tokens:, :]
    for i in range(1, sharers):
        to_sharer(i).start()
    settle_a()

    def rotate(field):
        return field * cosine[...] + pltpu.roll(field, HEAD_DIM // 2, 1) * sine[...]

    local_heads = block_a // HEAD_DIM
    queries = [
        rotate(total[:tokens, h * HEAD_DIM:(h + 1) * HEAD_DIM] * tensor_scales[0]).astype(BF16)
        for h in range(local_heads)
    ]
    for i in range(1, sharers):
        from_sharer(i).wait_recv()
    for q in range(sharers):
        for i in range(fold):
            rows = slice(q * share_rows + i * extra, q * share_rows + (i + 1) * extra)
            first = i * 2 * HEAD_DIM
            keys[rows, :] = kv_all[q, :, first:first + HEAD_DIM]
            values[rows, :] = kv_all[q, :, first + HEAD_DIM:first + 2 * HEAD_DIM]
    key_rows = rotate(keys[...] * tensor_scales[1]).astype(BF16)
    value_rows = (values[...] * tensor_scales[2]).astype(BF16)
    causal = lax.broadcasted_iota(jnp.int32, (tokens, tokens), 0) >= lax.broadcasted_iota(
        jnp.int32, (tokens, tokens), 1
    )
    for h in range(local_heads):
        scores = lax.dot_general(
            queries[h], key_rows, (((1,), (1,)), ((), ())), preferred_element_type=F32
        ) / math.sqrt(HEAD_DIM)
        scores = jnp.where(causal, scores, -1e30)
        top = jnp.max(scores, axis=-1, keepdims=True)
        expo = jnp.exp(scores - top)
        weights = (expo / jnp.sum(expo, axis=-1, keepdims=True)).astype(BF16)
        mixed[:, h * HEAD_DIM:(h + 1) * HEAD_DIM] = jnp.dot(
            weights, value_rows, preferred_element_type=F32
        ).astype(BF16)
    for i in range(1, sharers):
        to_sharer(i).wait_send()

    def multiply_b(t, dest):
        columns = pl.ds(pl.multiple_of(dest * block_b, block_b), block_b)
        acc[:tokens, :block_b] = jnp.dot(mixed[...], out_weight[:, columns], preferred_element_type=F32)

    summed, settle_b = reduce_scatter(
        multiply_b, 0, block_b, lambda j: None,
        (b_send, b_recv, b_ysend, b_yrecv, b_own, b_zrecv, b_ss, b_sr, b_ys, b_yr, b_zs, b_zr),
    )
    out[...] = (summed[...] * tensor_scales[3]).astype(BF16)
    settle_b()


def on_device(
    hidden_in, query_values, query_scales, pair_values, pair_scales, output_values, output_scales, tensor_scales
):
    devices = lax.axis_size("wide")
    rows_y = 2 if devices == 16 else 1
    length = devices // (2 * rows_y)
    cells = length * rows_y
    tokens, depth = hidden_in.shape
    block_a = query_values.shape[1] // devices
    block_b = output_values.shape[1] // devices
    sharers = devices // KV_HEADS
    extra = tokens // sharers // (block_a // (2 * HEAD_DIM))
    cosine, sine = rotary_tables(tokens)
    dma = pltpu.SemaphoreType.DMA

    def buffers(below, width, sibling_type):
        rows, wire = tokens + below, tokens + 2 * below
        return [
            pltpu.VMEM((SIBLING_SLOTS, rows, width), sibling_type),
            pltpu.VMEM((cells, rows, width), sibling_type),
            pltpu.VMEM((length, wire, width) if rows_y == 2 else (1, 16, 128), BF16),
            pltpu.VMEM((length, wire, width), BF16),
            pltpu.VMEM((length, rows, width), F32),
            pltpu.VMEM((length + 1, wire, width), BF16),
            dma((SIBLING_SLOTS,)), dma((cells,)), dma((length,)), dma((length,)),
            dma((length,)), dma((length + 1,)),
        ]

    anywhere = pl.BlockSpec(memory_space=pl.ANY)
    vmem = pl.BlockSpec(memory_space=pltpu.VMEM)
    features = query_values.shape[1] + pair_values.shape[1]
    return pl.pallas_call(
        functools.partial(block_kernel, devices, length, rows_y),
        out_shape=jax.ShapeDtypeStruct((tokens, block_b), BF16),
        in_specs=[vmem] + [anywhere] * 6 + [pl.BlockSpec(memory_space=pltpu.SMEM), vmem, vmem],
        out_specs=vmem,
        scratch_shapes=[
            pltpu.VMEM((TILES, depth, block_a), BF16),
            pltpu.VMEM((TILES, depth // 16, block_a), F32),
            dma((TILES,)), dma((TILES,)),
            pltpu.VMEM((depth, max(block_a, 256)), BF16),
            pltpu.VMEM((tokens + extra, max(block_a, block_b)), F32),
            pltpu.VMEM(pair_values.shape, BF16),
            pltpu.VMEM(pair_scales.shape, F32),
            dma((2,)),
            pltpu.VMEM((KV_HEADS, tokens, 2 * HEAD_DIM), F32),
            pltpu.VMEM(output_values.shape, BF16),
            pltpu.VMEM(output_scales.shape, F32),
            dma((2, length)),
        ]
        + buffers(extra, block_a, F32)
        + buffers(0, block_b, BF16)
        + [
            pltpu.VMEM((sharers, extra, block_a), F32),
            dma((sharers,)), dma((sharers,)),
            pltpu.VMEM((tokens, HEAD_DIM), F32),
            pltpu.VMEM((tokens, HEAD_DIM), F32),
            pltpu.VMEM((tokens, block_a), BF16),
        ],
        compiler_params=pltpu.CompilerParams(
            collective_id=0, has_side_effects=True, vmem_limit_bytes=63 * 1024 * 1024
        ),
        cost_estimate=pl.CostEstimate(
            flops=2 * tokens * (depth * features + output_values.size),
            bytes_accessed=2 * (query_values.size + pair_values.size + output_values.size),
            transcendentals=tokens * tokens * (block_a // HEAD_DIM),
        ),
    )(
        hidden_in, query_values, query_scales, pair_values, pair_scales, output_values, output_scales,
        tensor_scales, jnp.asarray(cosine), jnp.asarray(sine),
    )


def solution(mesh):
    in_specs = (P("groups", "wide"),) + (P("wide", None),) * 6 + (P(),)
    return jax.shard_map(
        on_device, mesh=mesh, in_specs=in_specs, out_specs=P("groups", "wide"), check_vma=False
    )
```
